32 devices in a mesh: cfg: 2 (over core), row: 4 (over z), col: 4 (over y, x).
Axes of the slice: x: 2, y: 2, z: 4, core: 2. Of those that a mesh axis runs over, the one named last changes fastest.
Arguments:
- img_tokens: bfloat16 [2, 4, 1024, 3072], P('cfg', 'col', None, 'row'), may hold values from -6 to 6
- txt_tokens: bfloat16 [2, 4, 512, 3072], P('cfg', 'col', None, 'row'), may hold values from -6 to 6
- img_mod: bfloat16 [2, 4, 2, 3072], P('cfg', 'col', None, 'row'), may hold values from -3 to 3
- txt_mod: bfloat16 [2, 4, 2, 3072], P('cfg', 'col', None, 'row'), may hold values from -3 to 3
- img_gate: bfloat16 [2, 4, 3072], P('cfg', 'col', 'row'), may hold values from -16 to 16
- txt_len: int32 [2, 4], P('cfg', 'col'), may hold values from 128 to 512, as said below
- img_qkv_weight: bfloat16 [3072, 3, 3072], P('col', None, 'row'), may hold values from -0.109375 to 0.109375
- txt_kv_weight: bfloat16 [3072, 2, 3072], P('col', None, 'row'), may hold values from -0.109375 to 0.109375
- out_weight: bfloat16 [3072, 3072], P('row', 'col'), may hold values from -0.109375 to 0.109375
- final_weight: bfloat16 [3072, 64], P('row'), may hold values from -0.109375 to 0.109375
- latent: float32 [4, 1024, 64], P('col', ('cfg', 'row')), may hold values from -6 to 6
- sigmas: float32 [5], replicated, may hold values from 0 to 2, as said below
- step_index: int32 [1], replicated, may hold values from 0 to 3
- guidance: float32 [1], replicated, may hold values from 1.5 to 5
Outputs:
- img_out: bfloat16 [2, 4, 1024, 3072], P('cfg', 'col', None, 'row')
- latent_next: float32 [4, 1024, 64], P('col', ('cfg', 'row'))
The draws below stay inside these ranges and needn't reach their ends.
Inputs may be any that keep to these rules, and one draw needn't show every extreme that they name: `txt_len`: in each half some prompt has all 512 text slots live and some other prompt exactly 128. `sigmas`: falls strictly along the table.
All inputs are finite; a program needn't handle non-finite values.
Results may differ from the reference program's by a relative error of at most 0.015.
Values may be sent and summed in bfloat16 or wider, within the bound.
A program may use at most 128 MiB of HBM per device.

```python
import math
import jax
import jax.numpy as jnp
from jax import lax

D = 3072
HEADS = 24
HD = 128
C = 64
IMG = 1024
TXT = 512
STEPS = 4
P_SIZE = 4
N_ROW = 4


def draw_txt_len(key, part):
    lengths = jax.random.randint(key, (2, P_SIZE), TXT // 4, TXT + 1)
    top_slot = jax.random.randint(jax.random.fold_in(key, 1), (2, 1), 0, P_SIZE)
    step_over = jax.random.randint(jax.random.fold_in(key, 2), (2, 1), 1, P_SIZE)
    low_slot = (top_slot + step_over) % P_SIZE
    slots = jnp.arange(P_SIZE, dtype=jnp.int32)[None, :]
    lengths = jnp.where(slots == top_slot, TXT, lengths)
    lengths = jnp.where(slots == low_slot, TXT // 4, lengths)
    return lengths.astype(jnp.int32)


def draw_sigmas(key, part):
    jitter = 0.5 * jax.random.uniform(key, (STEPS + 1,), jnp.float32)
    levels = jnp.arange(STEPS + 1, dtype=jnp.float32)
    return ((STEPS - levels + jitter) / STEPS).astype(jnp.float32)


def block_levels(key, shape, shards, least, high):
    level = 1.0
    for position, parts in shards:
        steps = jax.random.uniform(jax.random.fold_in(jax.random.fold_in(key, 6), position), (parts,), jnp.float32, least / len(shards), high / len(shards))
        level = level * jnp.repeat(jnp.exp(steps), shape[position] // parts).reshape((-1,) + (1,) * (len(shape) - 1 - position))
    return level


def bell_draw(key, shape, width, reach, pieces=(), kind=jnp.bfloat16):
    level = block_levels(key, shape, pieces, -0.22, 0.18) if pieces else 1.0
    drawn = jax.random.normal(key, shape, jnp.float32) * width * level
    return jnp.minimum(jnp.maximum(drawn, -reach), reach).astype(kind)


def setup_inputs(seed: int = 0) -> dict:
    key_of = jax.random.split(jax.random.key(seed), 15)
    img_tokens = bell_draw(key_of[0], (2, P_SIZE, IMG, D), 1.0, 6.0, ((0, 2), (1, 4), (3, 4)))
    txt_tokens = bell_draw(key_of[1], (2, P_SIZE, TXT, D), 1.0, 6.0, ((0, 2), (1, 4), (3, 4)))
    img_mod = bell_draw(key_of[2], (2, P_SIZE, 2, D), 0.5, 3.0, ((0, 2), (1, 4), (3, 4)))
    txt_mod = bell_draw(key_of[3], (2, P_SIZE, 2, D), 0.5, 3.0, ((0, 2), (1, 4), (3, 4)))
    img_gate = bell_draw(key_of[4], (2, P_SIZE, D), 4.0, 16.0, ((0, 2), (1, 4), (2, 4)))
    txt_len = draw_txt_len(jax.random.fold_in(key_of[14], 71), 0)
    img_qkv_weight = bell_draw(key_of[6], (D, 3, D), D ** -0.5, 0.109375, ((0, 4), (2, 4)))
    txt_kv_weight = bell_draw(key_of[7], (D, 2, D), D ** -0.5, 0.109375, ((0, 4), (2, 4)))
    out_weight = bell_draw(key_of[8], (D, D), D ** -0.5, 0.109375, ((0, 4), (1, 4)))
    final_weight = bell_draw(key_of[9], (D, C), D ** -0.5, 0.109375, ((0, 4),))
    latent = bell_draw(key_of[10], (P_SIZE, IMG, C), 1.0, 6.0, ((0, 4), (1, 8)), jnp.float32)
    sigmas = draw_sigmas(jax.random.fold_in(key_of[14], 71), 0)
    step_index = jax.random.randint(key_of[12], (1,), 0, STEPS).astype(jnp.int32)
    guidance = jnp.clip(jax.random.uniform(key_of[13], (1,), jnp.float32, 1.5, 5.0), 1.5, 5.0)
    return {"img_tokens": img_tokens, "txt_tokens": txt_tokens, "img_mod": img_mod, "txt_mod": txt_mod, "img_gate": img_gate, "txt_len": txt_len, "img_qkv_weight": img_qkv_weight, "txt_kv_weight": txt_kv_weight, "out_weight": out_weight, "final_weight": final_weight, "latent": latent, "sigmas": sigmas, "step_index": step_index, "guidance": guidance}


def modulate(tokens, shift_scale):
    values = tokens.astype(jnp.float32)
    centre = values - lax.optimization_barrier(jnp.mean(values, -1, keepdims=True))
    spread = lax.optimization_barrier(jnp.mean(centre * centre, -1, keepdims=True))
    normed = centre * lax.rsqrt(spread + 1e-06)
    scaled = normed * (1.0 + shift_scale[..., 1:2, :].astype(jnp.float32))
    return (scaled + shift_scale[..., 0:1, :].astype(jnp.float32)).astype(jnp.bfloat16)

def rms_norm(values):
    return values * lax.rsqrt(lax.optimization_barrier(jnp.mean(values * values, -1, keepdims=True)) + 1e-06)

def reference(img_tokens, txt_tokens, img_mod, txt_mod, img_gate, txt_len, img_qkv_weight, txt_kv_weight, out_weight, final_weight, latent, sigmas, step_index, guidance):

    def one_prompt(items):
        tokens, texts, img_shift, txt_shift, gating, length = items
        img_ready = modulate(tokens, img_shift)
        txt_ready = modulate(texts, txt_shift)
        img_proj = jnp.dot(img_ready, img_qkv_weight.reshape(D, 3 * D), preferred_element_type=jnp.float32)
        img_proj = img_proj.reshape(IMG, 3, HEADS, HD)
        txt_proj = jnp.dot(txt_ready, txt_kv_weight.reshape(D, 2 * D), preferred_element_type=jnp.float32)
        txt_proj = txt_proj.reshape(TXT, 2, HEADS, HD)
        queries = rms_norm(img_proj[:, 0]).astype(jnp.bfloat16)
        key_rows = jnp.concatenate([rms_norm(txt_proj[:, 0]), rms_norm(img_proj[:, 1])], 0).astype(jnp.bfloat16)
        value_rows = jnp.concatenate([txt_proj[:, 1], img_proj[:, 2]], 0).astype(jnp.bfloat16)
        scores = jnp.einsum('qhe,khe->hqk', queries.astype(jnp.float32), key_rows.astype(jnp.float32)) / math.sqrt(HD)
        positions = jnp.arange(TXT + IMG, dtype=jnp.int32)
        usable = (positions < length) | (positions >= TXT)
        weights = jnp.where(usable, jnp.exp(scores), 0.0)
        chances = (weights / lax.optimization_barrier(jnp.sum(weights, -1, keepdims=True))).astype(jnp.bfloat16)
        attended = jnp.einsum('hqk,khe->qhe', chances.astype(jnp.float32), value_rows.astype(jnp.float32))
        attended = attended.reshape(IMG, D).astype(jnp.bfloat16)
        group_width = D // N_ROW
        terms = jnp.einsum('inr,nrd->nid', attended.reshape(IMG, N_ROW, group_width).astype(jnp.float32), out_weight.reshape(N_ROW, group_width, D).astype(jnp.float32))
        projected = lax.optimization_barrier(jnp.sum(terms.astype(jnp.bfloat16).astype(jnp.float32), 0))
        img_out = (tokens.astype(jnp.float32) + gating[None, :].astype(jnp.float32) * projected).astype(jnp.bfloat16)
        velocity = jnp.dot(img_out, final_weight, preferred_element_type=jnp.float32)
        return (img_out, velocity)
    outputs = []
    speeds = []
    for half in range(2):
        img_out, velocity = lax.map(one_prompt, (img_tokens[half], txt_tokens[half], img_mod[half], txt_mod[half], img_gate[half], txt_len[half]))
        outputs.append(img_out)
        speeds.append(velocity)
    strength = guidance[0]
    guided = speeds[0] * (1.0 - strength) + speeds[1] * strength
    position_now = step_index[0]
    step_size = sigmas[position_now + 1] - sigmas[position_now]
    return (jnp.stack(outputs), latent + step_size * guided)
```

```python
import functools
import math

import jax
import jax.numpy as jnp
from jax import lax
from jax.experimental import pallas as pl
from jax.experimental.pallas import tpu as pltpu
from jax.sharding import PartitionSpec as P

HD = 128


def modulate(tokens, shift_scale):
    values = tokens.astype(jnp.float32)
    centre = values - jnp.mean(values, -1, keepdims=True)
    spread = jnp.mean(centre * centre, -1, keepdims=True)
    normed = centre * lax.rsqrt(spread + 1e-06)
    scaled = normed * (1.0 + shift_scale[..., 1:2, :].astype(jnp.float32))
    return (scaled + shift_scale[..., 0:1, :].astype(jnp.float32)).astype(jnp.bfloat16)


def rms_norm(values):
    return values * lax.rsqrt(jnp.mean(values * values, -1, keepdims=True) + 1e-06)


def add_rows(piece, ready):
    return jnp.dot(ready, piece.reshape(piece.shape[0], -1), preferred_element_type=jnp.float32)


def shards(
    img_tokens,
    txt_tokens,
    img_mod,
    txt_mod,
    img_gate,
    txt_len,
    img_qkv_weight,
    txt_kv_weight,
    out_weight,
    final_weight,
    latent,
    sigmas,
    step_index,
    guidance,
):
    img_whole, txt_whole, img_shift, txt_shift = (
        lax.all_gather(img_tokens, "row", axis=3, tiled=True),
        lax.all_gather(txt_tokens, "row", axis=3, tiled=True),
        lax.all_gather(img_mod, "row", axis=3, tiled=True),
        lax.all_gather(txt_mod, "row", axis=3, tiled=True),
    )
    prompts = img_tokens.shape[1]
    images = img_tokens.shape[2]
    text_slots = txt_tokens.shape[2]
    local_width = img_qkv_weight.shape[2]
    heads_here = local_width // HD
    img_ready = modulate(img_whole[0], img_shift[0]).reshape(prompts * images, -1)
    txt_ready = modulate(txt_whole[0], txt_shift[0]).reshape(prompts * text_slots, -1)
    img_proj = add_rows(lax.all_gather(img_qkv_weight, "col", axis=0, tiled=True), img_ready)
    txt_proj = add_rows(lax.all_gather(txt_kv_weight, "col", axis=0, tiled=True), txt_ready)
    img_proj = img_proj.reshape(prompts, images, 3, heads_here, HD)
    txt_proj = txt_proj.reshape(prompts, text_slots, 2, heads_here, HD)
    queries = rms_norm(img_proj[:, :, 0]).astype(jnp.bfloat16)
    key_rows = jnp.concatenate(
        [rms_norm(txt_proj[:, :, 0]), rms_norm(img_proj[:, :, 1])], 1
    ).astype(jnp.bfloat16)
    value_rows = jnp.concatenate([txt_proj[:, :, 1], img_proj[:, :, 2]], 1).astype(jnp.bfloat16)
    positions = jnp.arange(text_slots + images, dtype=jnp.int32)
    scores = jnp.einsum(
        "qhe,khe->hqk", queries[0], key_rows[0], preferred_element_type=jnp.float32
    ) / math.sqrt(HD)
    usable = (positions < txt_len[0, 0]) | (positions >= text_slots)
    weights = jnp.where(usable, jnp.exp(scores), 0.0)
    chances = (weights / jnp.sum(weights, -1, keepdims=True)).astype(jnp.bfloat16)
    mixed = jnp.einsum("hqk,khe->qhe", chances, value_rows[0], preferred_element_type=jnp.float32)
    outputs = mixed.reshape(images, local_width).astype(jnp.bfloat16)
    head_terms = jnp.dot(
        outputs,
        lax.all_gather(out_weight, "col", axis=1, tiled=True),
        preferred_element_type=jnp.float32,
    )
    projected = (
        lax.psum_scatter(head_terms.astype(jnp.bfloat16), "row", scatter_dimension=1, tiled=True)
        .astype(jnp.float32)
        .reshape(prompts, images, local_width)
    )
    gating = img_gate[0][:, None, :].astype(jnp.float32)
    img_out = (img_tokens[0].astype(jnp.float32) + gating * projected).astype(jnp.bfloat16)
    velocity = jnp.dot(
        img_out.reshape(prompts * images, local_width),
        final_weight,
        preferred_element_type=jnp.float32,
    )
    velocity = velocity.reshape(prompts, images, -1)
    strength = guidance[0]
    share = jnp.where(lax.axis_index("cfg") == 1, strength, 1.0 - strength)
    weighted = velocity * share
    halved = lax.psum_scatter(weighted.astype(jnp.bfloat16), "cfg", scatter_dimension=1, tiled=True)
    guided = lax.psum_scatter(halved, "row", scatter_dimension=1, tiled=True).astype(jnp.float32)
    position_now = step_index[0]
    step_size = sigmas[position_now + 1] - sigmas[position_now]
    return (img_out[None], latent + step_size * guided)


ROWS = 256
MESH = pl.DeviceIdType.MESH


def layer_kernel(
    scalars,
    live_len,
    img_hbm,
    txt_hbm,
    mods_hbm,
    gate,
    own_w,
    final_w,
    latent,
    out,
    latent_out,
    tok,
    weights,
    mods,
    ready,
    q_buf,
    k_buf,
    v_buf,
    from_up,
    from_down,
    mixed,
    vel_send,
    vel_recv,
    up_send,
    up_recv,
    dn_send,
    dn_recv,
    w_send,
    w_recv,
    m_send,
    m_recv,
    sum_dn_send,
    sum_dn_recv,
    sum_up_send,
    sum_up_recv,
    v_send,
    v_recv,
    local,
):
    g, r, c = lax.axis_index("cfg"), lax.axis_index("row"), lax.axis_index("col")
    n_row = 4
    last = n_row - 1
    images, width = img_hbm.shape
    texts = txt_hbm.shape[0]
    slots = images + texts
    txt_chunks, img_chunks = texts // ROWS, images // ROWS
    chunks = txt_chunks + img_chunks
    heads = width // HD
    half = width // 2
    beside_x = c + 1 - 2 * lax.rem(c, 2)
    beside_y = lax.rem(c + 2, 4)
    across = lax.rem(beside_x + 2, 4)
    sibling = (1 - g, r, c)
    me = g * n_row + r

    def peer(step):
        other = lax.rem(me + step, 2 * n_row)
        return other, (other // n_row, lax.rem(other, n_row), c)

    barrier = pltpu.get_barrier_semaphore()
    for step in range(1, 2 * n_row):
        pl.semaphore_signal(barrier, inc=1, device_id=peer(step)[1], device_id_type=MESH)
    for other in (beside_x, beside_y):
        pl.semaphore_signal(barrier, inc=1, device_id=(g, r, other), device_id_type=MESH)
    pl.semaphore_wait(barrier, 2 * n_row + 1)

    def remote(a, b, send, recv, where):
        return pltpu.make_async_remote_copy(
            src_ref=a, dst_ref=b, send_sem=send, recv_sem=recv, device_id=where, device_id_type=MESH
        )

    def tok_at(source, j):
        return tok.at[pl.ds(pl.multiple_of(source * slots + j * ROWS, ROWS), ROWS)]

    def own_chunk(j):
        if j < txt_chunks:
            return txt_hbm.at[pl.ds(j * ROWS, ROWS)]
        return img_hbm.at[pl.ds((j - txt_chunks) * ROWS, ROWS)]

    def up_copy(hops, j, a=None):
        b = tok_at(r - hops, j)
        return remote(b if a is None else a, b, up_send.at[hops, j], up_recv.at[hops, j], (g, r + 1, c))

    def dn_copy(hops, j, a=None):
        b = tok_at(r + hops, j)
        return remote(b if a is None else a, b, dn_send.at[hops, j], dn_recv.at[hops, j], (g, r - 1, c))

    def w_at(p, source, core):
        at = (p * 4 + source) * width + core * half
        return weights.at[pl.ds(pl.multiple_of(at, half), half)]

    def w_own(p):
        return own_w.at[pl.ds(pl.multiple_of(p * width + g * half, half), half)]

    def w_copy(p, i, a, b, where):
        return remote(a, b, w_send.at[p, i], w_recv.at[p, i], where)

    def to_x(p):
        return w_copy(p, 0, w_own(p), w_at(p, c, g), (g, r, beside_x))

    def to_y(p):
        return w_copy(p, 1, w_own(p), w_at(p, c, g), (g, r, beside_y))

    def onward(p):
        source = jnp.where(g == 0, beside_x, beside_y)
        target = jnp.where(g == 0, beside_y, beside_x)
        return w_copy(p, 2, w_at(p, source, g), w_at(p, source, g), (g, r, target))

    def share(p, i):
        source = (beside_x, beside_y, across)[i]
        return w_copy(p, 3 + i, w_at(p, source, g), w_at(p, source, g), sibling)

    def mods_copy(step):
        place = mods.at[pl.ds(pl.multiple_of(r * 16, 16), 16)]
        return remote(mods_hbm, place, m_send.at[step - 1], m_recv.at[step - 1], (g, lax.rem(r + step, n_row), c))

    for step in range(1, n_row):
        mods_copy(step).start()
    for j in range(chunks):

        @pl.when(r < last)
        def _():
            up_copy(0, j, own_chunk(j)).start()

        @pl.when(r > 0)
        def _():
            dn_copy(0, j, own_chunk(j)).start()

        if j < 6:
            to_x(j).start()
            to_y(j).start()

    locals_ = [
        pltpu.make_async_copy(txt_hbm, tok.at[pl.ds(pl.multiple_of(r * slots, ROWS), texts)], local.at[0]),
        pltpu.make_async_copy(img_hbm, tok.at[pl.ds(pl.multiple_of(r * slots + texts, ROWS), images)], local.at[1]),
        pltpu.make_async_copy(mods_hbm, mods.at[pl.ds(pl.multiple_of(r * 16, 16), 16)], local.at[2]),
    ]
    for p in range(6):
        locals_.append(
            pltpu.make_async_copy(
                own_w.at[pl.ds(p * width, width)],
                weights.at[pl.ds(pl.multiple_of((p * 4 + c) * width, width), width)],
                local.at[3 + p],
            )
        )
    for copy in locals_:
        copy.start()

    def arrive(hops, j):
        @pl.when(r > hops)
        def _():
            up_copy(hops, j).wait_recv()

        @pl.when(r < last - hops)
        def _():
            dn_copy(hops, j).wait_recv()

        if hops < n_row - 2:

            @pl.when((r > hops) & (r < last))
            def _():
                up_copy(hops + 1, j).start()

            @pl.when((r < last - hops) & (r > 0))
            def _():
                dn_copy(hops + 1, j).start()

    @pl.loop(0, chunks)
    def _(j):
        arrive(0, j)
        to_x(j).wait_recv()
        to_y(j).wait_recv()
        onward(j).start()
        share(j, 0).start()
        share(j, 1).start()

    @pl.loop(0, chunks)
    def _(j):
        arrive(1, j)
        onward(j).wait_recv()
        share(j, 2).start()

    for copy in locals_:
        copy.wait()
    for step in range(1, n_row):
        mods_copy(step).wait_recv()

    @pl.loop(0, chunks)
    def _(j):
        for i in range(3):
            share(j, i).wait_recv()

    def normalise(j, first):
        @pl.loop(0, ROWS // 32)
        def _(i):
            parts = []
            for s in range(n_row):
                rows = pl.ds(pl.multiple_of(s * slots + j * ROWS + i * 32, 32), 32)
                parts.append(tok[rows, :].astype(jnp.float32))
            total = sum(jnp.sum(x, -1, keepdims=True) for x in parts)
            mean = total / (n_row * width)
            parts = [x - mean for x in parts]
            spread = sum(jnp.sum(x * x, -1, keepdims=True) for x in parts) / (n_row * width)
            scale = lax.rsqrt(spread + 1e-06)
            for s in range(n_row):
                table = mods[pl.ds(s * 16, 16), :].astype(jnp.float32)
                value = parts[s] * scale * (1.0 + table[first + 1 : first + 2]) + table[first : first + 1]
                ready[pl.ds(pl.multiple_of(i * 32, 32), 32), pl.ds(s * width, width)] = value.astype(jnp.bfloat16)

    def project(p, put):
        @pl.loop(0, heads // 2)
        def _(t):
            block = weights[pl.ds(p * 4 * width, 4 * width), pl.ds(pl.multiple_of(t * 2 * HD, 2 * HD), 2 * HD)]
            y = jnp.dot(ready[...], block, preferred_element_type=jnp.float32)
            put(2 * t, y[:, :HD])
            put(2 * t + 1, y[:, HD:])

    def put_keys(at):
        def put(h, y):
            k_buf[h, pl.ds(at, ROWS), :] = rms_norm(y).astype(jnp.bfloat16)

        return put

    def put_values(at, alive):
        def put(h, y):
            v_buf[h, pl.ds(at, ROWS), pl.ds(0, HD)] = (y if alive is None else y * alive).astype(jnp.bfloat16)
            ones = jnp.ones((ROWS, HD), jnp.float32)
            v_buf[h, pl.ds(at, ROWS), pl.ds(HD, HD)] = (ones if alive is None else ones * alive).astype(jnp.bfloat16)

        return put

    @pl.loop(0, txt_chunks)
    def _(j):
        arrive(2, j)
        normalise(j, 2)
        at = pl.multiple_of(j * ROWS, ROWS)
        project(0, put_keys(at))
        place = at + lax.broadcasted_iota(jnp.int32, (ROWS, HD), 0)
        project(1, put_values(at, jnp.where(place < live_len[0], 1.0, 0.0)))

    q_scale = math.log2(math.e) / math.sqrt(HD)

    @pl.loop(0, img_chunks)
    def _(i):
        j = txt_chunks + i
        arrive(2, j)
        normalise(j, 0)
        at = pl.multiple_of(j * ROWS, ROWS)
        row = pl.multiple_of(i * ROWS, ROWS)
        project(2, put_keys(at))
        project(3, put_values(at, None))

        def put_queries(h, y):
            q_buf[h, pl.ds(row, ROWS), :] = (rms_norm(y) * q_scale).astype(jnp.bfloat16)

        project(4, put_queries)

    @pl.loop(0, 6)
    def _(p):
        to_x(p).wait_send()
        to_y(p).wait_send()
        onward(p).wait_send()
        for i in range(3):
            share(p, i).wait_send()

    def term_at(d, b):
        return pl.ds(pl.multiple_of(d * images + b * ROWS, ROWS), ROWS)

    def down_copy(d, b):
        return remote(
            weights.at[term_at(d, b)], from_up.at[term_at(d, b)], sum_dn_send.at[d, b], sum_dn_recv.at[d, b], (g, r - 1, c)
        )

    def upward_copy(d, b):
        return remote(
            weights.at[term_at(d, b)],
            from_down.at[term_at(d - 1, b)],
            sum_up_send.at[d - 1, b],
            sum_up_recv.at[d - 1, b],
            (g, r + 1, c),
        )

    @pl.loop(0, img_chunks)
    def _(b):
        row = pl.multiple_of(b * ROWS, ROWS)
        for h in range(heads):
            scores = lax.dot_general(
                q_buf[h, pl.ds(row, ROWS), :],
                k_buf[h],
                (((1,), (1,)), ((), ())),
                preferred_element_type=jnp.float32,
            )
            chances = jnp.exp2(scores).astype(jnp.bfloat16)
            y = jnp.dot(chances, v_buf[h], preferred_element_type=jnp.float32)
            mixed[:, pl.ds(h * HD, HD)] = (y[:, :HD] / y[:, HD:]).astype(jnp.bfloat16)

        @pl.loop(0, n_row)
        def _(d):
            block = weights[pl.ds(pl.multiple_of((20 + d) * width, width), width), :]
            y = jnp.dot(mixed[...], block, preferred_element_type=jnp.float32)
            weights[term_at(d, b), :] = y.astype(jnp.bfloat16)

        for i in range(last):

            @pl.when(r == last)
            def _():
                down_copy(i, b).start()

            @pl.when(r == 0)
            def _():
                upward_copy(last - i, b).start()

    strength = scalars[0]

    def finish(b, projected):
        own = tok[pl.ds(pl.multiple_of(r * slots + texts + b * ROWS, ROWS), ROWS), :].astype(jnp.float32)
        result = (own + gate[...].astype(jnp.float32) * projected).astype(jnp.bfloat16)
        rows = pl.ds(pl.multiple_of(b * ROWS, ROWS), ROWS)
        out[rows, :] = result
        velocity = jnp.dot(result, final_w[...], preferred_element_type=jnp.float32) * strength
        vel_send[rows, :] = velocity.astype(jnp.bfloat16)

    @pl.loop(0, img_chunks)
    def _(b):
        for i in range(last):
            d = i

            @pl.when((d < r) & (r < last))
            def _():
                down_copy(d, b).wait_recv()
                total = weights[term_at(d, b), :].astype(jnp.float32) + from_up[term_at(d, b), :].astype(jnp.float32)
                weights[term_at(d, b), :] = total.astype(jnp.bfloat16)
                down_copy(d, b).start()

            u = last - i

            @pl.when((u > r) & (r > 0))
            def _():
                upward_copy(u, b).wait_recv()
                total = weights[term_at(u, b), :].astype(jnp.float32) + from_down[term_at(u - 1, b), :].astype(jnp.float32)
                weights[term_at(u, b), :] = total.astype(jnp.bfloat16)
                upward_copy(u, b).start()

        @pl.when(r < last)
        def _():
            down_copy(r, b).wait_recv()
            total = weights[term_at(r, b), :].astype(jnp.float32) + from_up[term_at(r, b), :].astype(jnp.float32)

            @pl.when(r == 0)
            def _():
                finish(b, total)

            @pl.when(r > 0)
            def _():
                upward_copy(r, b).wait_recv()
                finish(b, total + from_down[term_at(r - 1, b), :].astype(jnp.float32))

        @pl.when(r == last)
        def _():
            upward_copy(r, b).wait_recv()
            finish(
                b, weights[term_at(r, b), :].astype(jnp.float32) + from_down[term_at(r - 1, b), :].astype(jnp.float32)
            )

    here = latent.shape[0]

    def vel_copy(step):
        other, where = peer(step)
        return remote(
            vel_send.at[pl.ds(pl.multiple_of(other * here, here), here)],
            vel_recv.at[pl.ds(step * here, here)],
            v_send.at[step - 1],
            v_recv.at[step - 1],
            where,
        )

    for step in range(1, 2 * n_row):
        vel_copy(step).start()
    guided = vel_send[pl.ds(pl.multiple_of(me * here, here), here), :].astype(jnp.float32)
    for step in range(1, 2 * n_row):
        vel_copy(step).wait_recv()
        guided += vel_recv[pl.ds(step * here, here), :].astype(jnp.float32)
    latent_out[...] = latent[...] + scalars[1] * guided[:, : latent.shape[1]]

    for step in range(1, 2 * n_row):
        vel_copy(step).wait_send()
    for step in range(1, n_row):
        mods_copy(step).wait_send()

    @pl.loop(0, chunks)
    def _(j):
        for hops in range(last):

            @pl.when((r >= hops) & (r < last))
            def _():
                up_copy(hops, j).wait_send()

            @pl.when((r <= last - hops) & (r > 0))
            def _():
                dn_copy(hops, j).wait_send()

    @pl.loop(0, img_chunks)
    def _(b):
        for i in range(last):

            @pl.when(i < r)
            def _():
                down_copy(i, b).wait_send()

            @pl.when(last - i > r)
            def _():
                upward_copy(last - i, b).wait_send()


def fused(
    img_tokens,
    txt_tokens,
    img_mod,
    txt_mod,
    img_gate,
    txt_len,
    img_qkv_weight,
    txt_kv_weight,
    out_weight,
    final_weight,
    latent,
    sigmas,
    step_index,
    guidance,
):
    images, width = img_tokens.shape[2:]
    texts = txt_tokens.shape[2]
    slots = images + texts
    heads = width // HD
    chunks = slots // ROWS
    blocks = images // ROWS
    strength = guidance[0]
    share = jnp.where(lax.axis_index("cfg") == 1, strength, 1.0 - strength)
    now = step_index[0]
    scalars = jnp.stack([share, sigmas[now + 1] - sigmas[now]])
    txt_w = jnp.transpose(txt_kv_weight, (1, 0, 2)).reshape(2 * width, width)
    img_w = jnp.transpose(img_qkv_weight, (1, 0, 2))
    own_w = jnp.concatenate([txt_w, img_w[1], img_w[2], img_w[0], out_weight], 0)
    mods = jnp.concatenate([img_mod[0, 0], txt_mod[0, 0], jnp.zeros((12, width), jnp.bfloat16)], 0)
    final_w = jnp.pad(final_weight, ((0, 0), (0, HD - final_weight.shape[1])))
    smem, vmem, anywhere = (
        pl.BlockSpec(memory_space=pltpu.SMEM),
        pl.BlockSpec(memory_space=pltpu.VMEM),
        pl.BlockSpec(memory_space=pl.ANY),
    )
    dma = pltpu.SemaphoreType.DMA
    here = latent.shape[1]
    out, latent_out = pl.pallas_call(
        layer_kernel,
        out_shape=(
            jax.ShapeDtypeStruct((images, width), jnp.bfloat16),
            jax.ShapeDtypeStruct(latent.shape[1:], jnp.float32),
        ),
        in_specs=[smem, smem, anywhere, anywhere, anywhere, vmem, anywhere, vmem, vmem],
        out_specs=(vmem, vmem),
        scratch_shapes=[
            pltpu.VMEM((4 * slots, width), jnp.bfloat16),
            pltpu.VMEM((24 * width, width), jnp.bfloat16),
            pltpu.VMEM((64, width), jnp.bfloat16),
            pltpu.VMEM((ROWS, 4 * width), jnp.bfloat16),
            pltpu.VMEM((heads, images, HD), jnp.bfloat16),
            pltpu.VMEM((heads, slots, HD), jnp.bfloat16),
            pltpu.VMEM((heads, slots, 2 * HD), jnp.bfloat16),
            pltpu.VMEM((3 * images, width), jnp.bfloat16),
            pltpu.VMEM((3 * images, width), jnp.bfloat16),
            pltpu.VMEM((ROWS, width), jnp.bfloat16),
            pltpu.VMEM((images, HD), jnp.bfloat16),
            pltpu.VMEM((8 * here, HD), jnp.bfloat16),
            dma((3, chunks)),
            dma((3, chunks)),
            dma((3, chunks)),
            dma((3, chunks)),
            dma((6, 6)),
            dma((6, 6)),
            dma((3,)),
            dma((3,)),
            dma((3, blocks)),
            dma((3, blocks)),
            dma((3, blocks)),
            dma((3, blocks)),
            dma((7,)),
            dma((7,)),
            dma((9,)),
        ],
        compiler_params=pltpu.CompilerParams(
            collective_id=0, has_side_effects=True, vmem_limit_bytes=63 * 1024 * 1024
        ),
    )(
        scalars,
        txt_len[0],
        img_tokens[0, 0],
        txt_tokens[0, 0],
        mods,
        img_gate[0],
        own_w,
        final_w,
        latent[0],
    )
    return out[None, None], latent_out[None]


def solution(mesh):
    return jax.shard_map(
        fused if mesh.shape["col"] == 4 and mesh.shape["row"] == 4 else shards,
        mesh=mesh,
        in_specs=(
            P("cfg", "col", None, "row"),
            P("cfg", "col", None, "row"),
            P("cfg", "col", None, "row"),
            P("cfg", "col", None, "row"),
            P("cfg", "col", "row"),
            P("cfg", "col"),
            P("col", None, "row"),
            P("col", None, "row"),
            P("row", "col"),
            P("row", None),
            P("col", ("cfg", "row"), None),
            P(),
            P(),
            P(),
        ),
        out_specs=(P("cfg", "col", None, "row"), P("col", ("cfg", "row"), None)),
        check_vma=False,
    )
```

```python
import functools
import math

import jax
import jax.numpy as jnp
from jax import lax
from jax.experimental import pallas as pl
from jax.experimental.pallas import tpu as pltpu
from jax.sharding import PartitionSpec as P

HD = 128


def modulate(tokens, shift_scale):
    values = tokens.astype(jnp.float32)
    centre = values - jnp.mean(values, -1, keepdims=True)
    spread = jnp.mean(centre * centre, -1, keepdims=True)
    normed = centre * lax.rsqrt(spread + 1e-06)
    scaled = normed * (1.0 + shift_scale[..., 1:2, :].astype(jnp.float32))
    return (scaled + shift_scale[..., 0:1, :].astype(jnp.float32)).astype(jnp.bfloat16)


def rms_norm(values):
    return values * lax.rsqrt(jnp.mean(values * values, -1, keepdims=True) + 1e-06)


def add_rows(piece, ready):
    return jnp.dot(ready, piece.reshape(piece.shape[0], -1), preferred_element_type=jnp.float32)


def shards(
    img_tokens,
    txt_tokens,
    img_mod,
    txt_mod,
    img_gate,
    txt_len,
    img_qkv_weight,
    txt_kv_weight,
    out_weight,
    final_weight,
    latent,
    sigmas,
    step_index,
    guidance,
):
    img_whole, txt_whole, img_shift, txt_shift = (
        lax.all_gather(img_tokens, "row", axis=3, tiled=True),
        lax.all_gather(txt_tokens, "row", axis=3, tiled=True),
        lax.all_gather(img_mod, "row", axis=3, tiled=True),
        lax.all_gather(txt_mod, "row", axis=3, tiled=True),
    )
    prompts = img_tokens.shape[1]
    images = img_tokens.shape[2]
    text_slots = txt_tokens.shape[2]
    local_width = img_qkv_weight.shape[2]
    heads_here = local_width // HD
    img_ready = modulate(img_whole[0], img_shift[0]).reshape(prompts * images, -1)
    txt_ready = modulate(txt_whole[0], txt_shift[0]).reshape(prompts * text_slots, -1)
    img_proj = add_rows(lax.all_gather(img_qkv_weight, "col", axis=0, tiled=True), img_ready)
    txt_proj = add_rows(lax.all_gather(txt_kv_weight, "col", axis=0, tiled=True), txt_ready)
    img_proj = img_proj.reshape(prompts, images, 3, heads_here, HD)
    txt_proj = txt_proj.reshape(prompts, text_slots, 2, heads_here, HD)
    queries = rms_norm(img_proj[:, :, 0]).astype(jnp.bfloat16)
    key_rows = jnp.concatenate(
        [rms_norm(txt_proj[:, :, 0]), rms_norm(img_proj[:, :, 1])], 1
    ).astype(jnp.bfloat16)
    value_rows = jnp.concatenate([txt_proj[:, :, 1], img_proj[:, :, 2]], 1).astype(jnp.bfloat16)
    positions = jnp.arange(text_slots + images, dtype=jnp.int32)
    scores = jnp.einsum(
        "qhe,khe->hqk", queries[0], key_rows[0], preferred_element_type=jnp.float32
    ) / math.sqrt(HD)
    usable = (positions < txt_len[0, 0]) | (positions >= text_slots)
    weights = jnp.where(usable, jnp.exp(scores), 0.0)
    chances = (weights / jnp.sum(weights, -1, keepdims=True)).astype(jnp.bfloat16)
    mixed = jnp.einsum("hqk,khe->qhe", chances, value_rows[0], preferred_element_type=jnp.float32)
    outputs = mixed.reshape(images, local_width).astype(jnp.bfloat16)
    head_terms = jnp.dot(
        outputs,
        lax.all_gather(out_weight, "col", axis=1, tiled=True),
        preferred_element_type=jnp.float32,
    )
    projected = (
        lax.psum_scatter(head_terms.astype(jnp.bfloat16), "row", scatter_dimension=1, tiled=True)
        .astype(jnp.float32)
        .reshape(prompts, images, local_width)
    )
    gating = img_gate[0][:, None, :].astype(jnp.float32)
    img_out = (img_tokens[0].astype(jnp.float32) + gating * projected).astype(jnp.bfloat16)
    velocity = jnp.dot(
        img_out.reshape(prompts * images, local_width),
        final_weight,
        preferred_element_type=jnp.float32,
    )
    velocity = velocity.reshape(prompts, images, -1)
    strength = guidance[0]
    share = jnp.where(lax.axis_index("cfg") == 1, strength, 1.0 - strength)
    weighted = velocity * share
    halved = lax.psum_scatter(weighted.astype(jnp.bfloat16), "cfg", scatter_dimension=1, tiled=True)
    guided = lax.psum_scatter(halved, "row", scatter_dimension=1, tiled=True).astype(jnp.float32)
    position_now = step_index[0]
    step_size = sigmas[position_now + 1] - sigmas[position_now]
    return (img_out[None], latent + step_size * guided)


ROWS = 256
AHEAD = 3
MESH = pl.DeviceIdType.MESH


def layer_kernel(
    scalars,
    live_len,
    img_hbm,
    txt_hbm,
    mods_hbm,
    gate,
    own_w,
    final_w,
    latent,
    out,
    latent_out,
    tok,
    weights,
    mods,
    q_buf,
    k_buf,
    v_buf,
    from_up,
    from_down,
    mixed,
    vel_send,
    vel_recv,
    up_send,
    up_recv,
    dn_send,
    dn_recv,
    w_send,
    w_recv,
    m_send,
    m_recv,
    sum_dn_send,
    sum_dn_recv,
    sum_up_send,
    sum_up_recv,
    v_send,
    v_recv,
    local,
    go,
):
    g, r, c = lax.axis_index("cfg"), lax.axis_index("row"), lax.axis_index("col")
    n_row = 4
    last = n_row - 1
    images, width = img_hbm.shape
    texts = txt_hbm.shape[0]
    slots = images + texts
    txt_chunks, img_chunks = texts // ROWS, images // ROWS
    chunks = txt_chunks + img_chunks
    heads = width // HD
    half = width // 2
    beside_x = c + 1 - 2 * lax.rem(c, 2)
    beside_y = lax.rem(c + 2, 4)
    across = lax.rem(beside_x + 2, 4)
    sibling = (1 - g, r, c)
    me = g * n_row + r

    def peer(step):
        other = lax.rem(me + step, 2 * n_row)
        return other, (other // n_row, lax.rem(other, n_row), c)

    barrier = pltpu.get_barrier_semaphore()
    for step in range(1, 2 * n_row):
        pl.semaphore_signal(barrier, inc=1, device_id=peer(step)[1], device_id_type=MESH)
    for other in (beside_x, beside_y):
        pl.semaphore_signal(barrier, inc=1, device_id=(g, r, other), device_id_type=MESH)
    pl.semaphore_wait(barrier, 2 * n_row + 1)

    def remote(a, b, send, recv, where):
        return pltpu.make_async_remote_copy(
            src_ref=a, dst_ref=b, send_sem=send, recv_sem=recv, device_id=where, device_id_type=MESH
        )

    def tok_at(source, j):
        return tok.at[pl.ds(pl.multiple_of(source * slots + j * ROWS, ROWS), ROWS)]

    def own_chunk(j):
        if j < txt_chunks:
            return txt_hbm.at[pl.ds(j * ROWS, ROWS)]
        return img_hbm.at[pl.ds((j - txt_chunks) * ROWS, ROWS)]

    def up_copy(hops, j, a=None):
        b = tok_at(r - hops, j)
        return remote(b if a is None else a, b, up_send.at[hops, j], up_recv.at[hops, j], (g, r + 1, c))

    def dn_copy(hops, j, a=None):
        b = tok_at(r + hops, j)
        return remote(b if a is None else a, b, dn_send.at[hops, j], dn_recv.at[hops, j], (g, r - 1, c))

    def w_at(p, source, core):
        at = (p * 4 + source) * width + core * half
        return weights.at[pl.ds(pl.multiple_of(at, half), half)]

    def w_own(p):
        return own_w.at[pl.ds(pl.multiple_of(p * width + g * half, half), half)]

    def w_copy(p, i, a, b, where):
        return remote(a, b, w_send.at[p, i], w_recv.at[p, i], where)

    def to_x(p):
        return w_copy(p, 0, w_own(p), w_at(p, c, g), (g, r, beside_x))

    def to_y(p):
        return w_copy(p, 1, w_own(p), w_at(p, c, g), (g, r, beside_y))

    def onward(p):
        source = jnp.where(g == 0, beside_x, beside_y)
        target = jnp.where(g == 0, beside_y, beside_x)
        return w_copy(p, 2, w_at(p, source, g), w_at(p, source, g), (g, r, target))

    def share(p, i):
        source = (beside_x, beside_y, across)[i]
        return w_copy(p, 3 + i, w_at(p, source, g), w_at(p, source, g), sibling)

    def mods_copy(step):
        place = mods.at[pl.ds(pl.multiple_of(r * 16, 16), 16)]
        return remote(mods_hbm, place, m_send.at[step - 1], m_recv.at[step - 1], (g, lax.rem(r + step, n_row), c))

    for step in range(1, n_row):
        mods_copy(step).start()
    for p in range(AHEAD):
        to_x(p).start()
        to_y(p).start()

    def start_own():
        for j in range(chunks):

            @pl.when(r < last)
            def _():
                up_copy(0, j, own_chunk(j)).start()

            @pl.when(r > 0)
            def _():
                dn_copy(0, j, own_chunk(j)).start()

    locals_ = [
        pltpu.make_async_copy(txt_hbm, tok.at[pl.ds(pl.multiple_of(r * slots, ROWS), texts)], local.at[0]),
        pltpu.make_async_copy(img_hbm, tok.at[pl.ds(pl.multiple_of(r * slots + texts, ROWS), images)], local.at[1]),
        pltpu.make_async_copy(mods_hbm, mods.at[pl.ds(pl.multiple_of(r * 16, 16), 16)], local.at[2]),
        pltpu.make_async_copy(img_hbm, out, local.at[9]),
    ]
    for p in range(6):
        locals_.append(
            pltpu.make_async_copy(
                own_w.at[pl.ds(p * width, width)],
                weights.at[pl.ds(pl.multiple_of((p * 4 + c) * width, width), width)],
                local.at[3 + p],
            )
        )
    for copy in locals_:
        copy.start()

    def arrive(hops, j):
        @pl.when(r > hops)
        def _():
            up_copy(hops, j).wait_recv()

        @pl.when(r < last - hops)
        def _():
            dn_copy(hops, j).wait_recv()

        if hops < n_row - 2:

            @pl.when((r > hops) & (r < last))
            def _():
                up_copy(hops + 1, j).start()

            @pl.when((r < last - hops) & (r > 0))
            def _():
                dn_copy(hops + 1, j).start()

    def arrivals(hops, low, high):
        @pl.loop(low, high)
        def _(j):
            arrive(hops, j)

    def direct(p):
        to_x(p).wait_recv()
        to_y(p).wait_recv()
        if p + AHEAD < 6:
            to_x(p + AHEAD).start()
            to_y(p + AHEAD).start()
        onward(p).start()
        share(p, 0).start()
        share(p, 1).start()

    def diagonal(p):
        onward(p).wait_recv()
        share(p, 2).start()

    def have(p):
        for i in range(3):
            share(p, i).wait_recv()

    @pl.when(g == 0)
    def _():
        start_own()
        arrivals(0, 0, chunks)
        direct(0)
        arrivals(1, 0, chunks // 2)
        direct(1)
        diagonal(0)
        arrivals(1, chunks // 2, chunks)
        direct(2)
        diagonal(1)
        arrivals(2, 0, txt_chunks)
        pl.semaphore_signal(go, inc=1, device_id=(1, r, c), device_id_type=MESH)

    @pl.when(g == 1)
    def _():
        for p in range(6):
            direct(p)
            if p:
                diagonal(p - 1)
        diagonal(5)
        pl.semaphore_wait(go, 1)
        start_own()
        arrivals(0, 0, chunks)
        arrivals(1, 0, chunks)
        arrivals(2, 0, txt_chunks)

    for copy in locals_:
        copy.wait()
    for step in range(1, n_row):
        mods_copy(step).wait_recv()
    have(0)
    have(1)

    def passed_on(j):
        for hops in range(1, last):

            @pl.when((r >= hops) & (r < last))
            def _():
                up_copy(hops, j).wait_send()

            @pl.when((r <= last - hops) & (r > 0))
            def _():
                dn_copy(hops, j).wait_send()

    def normalise(j, first):
        passed_on(j)

        @pl.loop(0, ROWS // 32)
        def _(i):
            parts = []
            for s in range(n_row):
                rows = pl.ds(pl.multiple_of(s * slots + j * ROWS + i * 32, 32), 32)
                parts.append(tok[rows, :].astype(jnp.float32))
            total = sum(jnp.sum(x, -1, keepdims=True) for x in parts)
            mean = total / (n_row * width)
            parts = [x - mean for x in parts]
            spread = sum(jnp.sum(x * x, -1, keepdims=True) for x in parts) / (n_row * width)
            scale = lax.rsqrt(spread + 1e-06)
            for s in range(n_row):
                table = mods[pl.ds(s * 16, 16), :].astype(jnp.float32)
                value = parts[s] * scale * (1.0 + table[first + 1 : first + 2]) + table[first : first + 1]
                rows = pl.ds(pl.multiple_of(s * slots + j * ROWS + i * 32, 32), 32)
                tok[rows, :] = value.astype(jnp.bfloat16)

    def project(p, j, put):
        @pl.loop(0, heads // 2)
        def _(t):
            columns = pl.ds(pl.multiple_of(t * 2 * HD, 2 * HD), 2 * HD)
            y = sum(
                jnp.dot(
                    tok_at(s, j)[...],
                    weights[pl.ds((p * 4 + s) * width, width), columns],
                    preferred_element_type=jnp.float32,
                )
                for s in range(n_row)
            )
            put(2 * t, y[:, :HD])
            put(2 * t + 1, y[:, HD:])

    def put_keys(at):
        def put(h, y):
            k_buf[h, pl.ds(at, ROWS), :] = rms_norm(y).astype(jnp.bfloat16)

        return put

    def put_values(at, alive):
        def put(h, y):
            v_buf[h, pl.ds(at, ROWS), pl.ds(0, HD)] = (y if alive is None else y * alive).astype(jnp.bfloat16)
            ones = jnp.ones((ROWS, HD), jnp.float32)
            v_buf[h, pl.ds(at, ROWS), pl.ds(HD, HD)] = (ones if alive is None else ones * alive).astype(jnp.bfloat16)

        return put

    @pl.loop(0, txt_chunks)
    def _(j):
        normalise(j, 2)
        at = pl.multiple_of(j * ROWS, ROWS)
        project(0, j, put_keys(at))
        place = at + lax.broadcasted_iota(jnp.int32, (ROWS, HD), 0)
        project(1, j, put_values(at, jnp.where(place < live_len[0], 1.0, 0.0)))

    q_scale = math.log2(math.e) / math.sqrt(HD)

    def keys(j):
        project(2, j, put_keys(pl.multiple_of(j * ROWS, ROWS)))

    def values(j):
        project(3, j, put_values(pl.multiple_of(j * ROWS, ROWS), None))

    def queries(j):
        row = pl.multiple_of((j - txt_chunks) * ROWS, ROWS)

        def put(h, y):
            q_buf[h, pl.ds(row, ROWS), :] = (rms_norm(y) * q_scale).astype(jnp.bfloat16)

        project(4, j, put)

    def image_in(j):
        arrive(2, j)
        normalise(j, 0)

    def image_rows(*steps):
        @pl.loop(txt_chunks, chunks)
        def _(j):
            for step in steps:
                step(j)

    @pl.when(g == 0)
    def _():
        direct(3)
        diagonal(2)
        image_rows(image_in)
        have(2)
        image_rows(keys)
        direct(4)
        diagonal(3)
        have(3)
        image_rows(values)
        direct(5)
        diagonal(4)
        have(4)
        image_rows(queries)
        diagonal(5)
        have(5)

    @pl.when(g == 1)
    def _():
        for p in range(2, 6):
            have(p)
        image_rows(image_in, keys, values, queries)

    @pl.loop(0, 6)
    def _(p):
        to_x(p).wait_send()
        to_y(p).wait_send()
        onward(p).wait_send()
        for i in range(3):
            share(p, i).wait_send()

    def term_at(d, b):
        return pl.ds(pl.multiple_of(d * images + b * ROWS, ROWS), ROWS)

    def down_copy(d, b):
        return remote(
            weights.at[term_at(d, b)], from_up.at[term_at(d, b)], sum_dn_send.at[d, b], sum_dn_recv.at[d, b], (g, r - 1, c)
        )

    def upward_copy(d, b):
        return remote(
            weights.at[term_at(d, b)],
            from_down.at[term_at(d - 1, b)],
            sum_up_send.at[d - 1, b],
            sum_up_recv.at[d - 1, b],
            (g, r + 1, c),
        )

    @pl.loop(0, img_chunks)
    def _(b):
        row = pl.multiple_of(b * ROWS, ROWS)
        for h in range(heads):
            scores = lax.dot_general(
                q_buf[h, pl.ds(row, ROWS), :],
                k_buf[h],
                (((1,), (1,)), ((), ())),
                preferred_element_type=jnp.float32,
            )
            chances = jnp.exp2(scores).astype(jnp.bfloat16)
            y = jnp.dot(chances, v_buf[h], preferred_element_type=jnp.float32)
            mixed[:, pl.ds(h * HD, HD)] = (y[:, :HD] / y[:, HD:]).astype(jnp.bfloat16)

        @pl.loop(0, n_row)
        def _(d):
            block = weights[pl.ds(pl.multiple_of((20 + d) * width, width), width), :]
            y = jnp.dot(mixed[...], block, preferred_element_type=jnp.float32)
            weights[term_at(d, b), :] = y.astype(jnp.bfloat16)

        for i in range(last):

            @pl.when(r == last)
            def _():
                down_copy(i, b).start()

            @pl.when(r == 0)
            def _():
                upward_copy(last - i, b).start()

    strength = scalars[0]

    def finish(b, projected):
        rows = pl.ds(pl.multiple_of(b * ROWS, ROWS), ROWS)
        own = out[rows, :].astype(jnp.float32)
        result = (own + gate[...].astype(jnp.float32) * projected).astype(jnp.bfloat16)
        out[rows, :] = result
        velocity = jnp.dot(result, final_w[...], preferred_element_type=jnp.float32) * strength
        vel_send[rows, :] = velocity.astype(jnp.bfloat16)

    @pl.loop(0, img_chunks)
    def _(b):
        for i in range(last):
            d = i

            @pl.when((d < r) & (r < last))
            def _():
                down_copy(d, b).wait_recv()
                total = weights[term_at(d, b), :].astype(jnp.float32) + from_up[term_at(d, b), :].astype(jnp.float32)
                weights[term_at(d, b), :] = total.astype(jnp.bfloat16)
                down_copy(d, b).start()

            u = last - i

            @pl.when((u > r) & (r > 0))
            def _():
                upward_copy(u, b).wait_recv()
                total = weights[term_at(u, b), :].astype(jnp.float32) + from_down[term_at(u - 1, b), :].astype(jnp.float32)
                weights[term_at(u, b), :] = total.astype(jnp.bfloat16)
                upward_copy(u, b).start()

        @pl.when(r < last)
        def _():
            down_copy(r, b).wait_recv()
            total = weights[term_at(r, b), :].astype(jnp.float32) + from_up[term_at(r, b), :].astype(jnp.float32)

            @pl.when(r == 0)
            def _():
                finish(b, total)

            @pl.when(r > 0)
            def _():
                upward_copy(r, b).wait_recv()
                finish(b, total + from_down[term_at(r - 1, b), :].astype(jnp.float32))

        @pl.when(r == last)
        def _():
            upward_copy(r, b).wait_recv()
            finish(
                b, weights[term_at(r, b), :].astype(jnp.float32) + from_down[term_at(r - 1, b), :].astype(jnp.float32)
            )

    here = latent.shape[0]

    def vel_copy(step):
        other, where = peer(step)
        return remote(
            vel_send.at[pl.ds(pl.multiple_of(other * here, here), here)],
            vel_recv.at[pl.ds(step * here, here)],
            v_send.at[step - 1],
            v_recv.at[step - 1],
            where,
        )

    for step in range(1, 2 * n_row):
        vel_copy(step).start()
    guided = vel_send[pl.ds(pl.multiple_of(me * here, here), here), :].astype(jnp.float32)
    for step in range(1, 2 * n_row):
        vel_copy(step).wait_recv()
        guided += vel_recv[pl.ds(step * here, here), :].astype(jnp.float32)
    latent_out[...] = latent[...] + scalars[1] * guided[:, : latent.shape[1]]

    for step in range(1, 2 * n_row):
        vel_copy(step).wait_send()
    for step in range(1, n_row):
        mods_copy(step).wait_send()

    @pl.loop(0, chunks)
    def _(j):
        @pl.when(r < last)
        def _():
            up_copy(0, j).wait_send()

        @pl.when(r > 0)
        def _():
            dn_copy(0, j).wait_send()

    @pl.loop(0, img_chunks)
    def _(b):
        for i in range(last):

            @pl.when(i < r)
            def _():
                down_copy(i, b).wait_send()

            @pl.when(last - i > r)
            def _():
                upward_copy(last - i, b).wait_send()


def fused(
    img_tokens,
    txt_tokens,
    img_mod,
    txt_mod,
    img_gate,
    txt_len,
    img_qkv_weight,
    txt_kv_weight,
    out_weight,
    final_weight,
    latent,
    sigmas,
    step_index,
    guidance,
):
    images, width = img_tokens.shape[2:]
    texts = txt_tokens.shape[2]
    slots = images + texts
    heads = width // HD
    chunks = slots // ROWS
    blocks = images // ROWS
    strength = guidance[0]
    share = jnp.where(lax.axis_index("cfg") == 1, strength, 1.0 - strength)
    now = step_index[0]
    scalars = jnp.stack([share, sigmas[now + 1] - sigmas[now]])
    txt_w = jnp.transpose(txt_kv_weight, (1, 0, 2)).reshape(2 * width, width)
    img_w = jnp.transpose(img_qkv_weight, (1, 0, 2))
    own_w = jnp.concatenate([txt_w, img_w[1], img_w[2], img_w[0], out_weight], 0)
    mods = jnp.concatenate([img_mod[0, 0], txt_mod[0, 0], jnp.zeros((12, width), jnp.bfloat16)], 0)
    final_w = jnp.pad(final_weight, ((0, 0), (0, HD - final_weight.shape[1])))
    smem, vmem, anywhere = (
        pl.BlockSpec(memory_space=pltpu.SMEM),
        pl.BlockSpec(memory_space=pltpu.VMEM),
        pl.BlockSpec(memory_space=pl.ANY),
    )
    dma = pltpu.SemaphoreType.DMA
    here = latent.shape[1]
    out, latent_out = pl.pallas_call(
        layer_kernel,
        out_shape=(
            jax.ShapeDtypeStruct((images, width), jnp.bfloat16),
            jax.ShapeDtypeStruct(latent.shape[1:], jnp.float32),
        ),
        in_specs=[smem, smem, anywhere, anywhere, anywhere, vmem, anywhere, vmem, vmem],
        out_specs=(vmem, vmem),
        scratch_shapes=[
            pltpu.VMEM((4 * slots, width), jnp.bfloat16),
            pltpu.VMEM((24 * width, width), jnp.bfloat16),
            pltpu.VMEM((64, width), jnp.bfloat16),
            pltpu.VMEM((heads, images, HD), jnp.bfloat16),
            pltpu.VMEM((heads, slots, HD), jnp.bfloat16),
            pltpu.VMEM((heads, slots, 2 * HD), jnp.bfloat16),
            pltpu.VMEM((3 * images, width), jnp.bfloat16),
            pltpu.VMEM((3 * images, width), jnp.bfloat16),
            pltpu.VMEM((ROWS, width), jnp.bfloat16),
            pltpu.VMEM((images, HD), jnp.bfloat16),
            pltpu.VMEM((8 * here, HD), jnp.bfloat16),
            dma((3, chunks)),
            dma((3, chunks)),
            dma((3, chunks)),
            dma((3, chunks)),
            dma((6, 6)),
            dma((6, 6)),
            dma((3,)),
            dma((3,)),
            dma((3, blocks)),
            dma((3, blocks)),
            dma((3, blocks)),
            dma((3, blocks)),
            dma((7,)),
            dma((7,)),
            dma((10,)),
            pltpu.SemaphoreType.REGULAR,
        ],
        compiler_params=pltpu.CompilerParams(
            collective_id=0, has_side_effects=True, vmem_limit_bytes=63 * 1024 * 1024
        ),
    )(
        scalars,
        txt_len[0],
        img_tokens[0, 0],
        txt_tokens[0, 0],
        mods,
        img_gate[0],
        own_w,
        final_w,
        latent[0],
    )
    return out[None, None], latent_out[None]


def solution(mesh):
    return jax.shard_map(
        fused if mesh.shape["col"] == 4 and mesh.shape["row"] == 4 else shards,
        mesh=mesh,
        in_specs=(
            P("cfg", "col", None, "row"),
            P("cfg", "col", None, "row"),
            P("cfg", "col", None, "row"),
            P("cfg", "col", None, "row"),
            P("cfg", "col", "row"),
            P("cfg", "col"),
            P("col", None, "row"),
            P("col", None, "row"),
            P("row", "col"),
            P("row", None),
            P("col", ("cfg", "row"), None),
            P(),
            P(),
            P(),
        ),
        out_specs=(P("cfg", "col", None, "row"), P("col", ("cfg", "row"), None)),
        check_vma=False,
    )
```
